256 devices in a mesh: segment: 32 (over x, z_lo, y), tp: 8 (over z_hi, core).
Axes of the slice: x: 4, y: 4, z: 8 (z_hi: 4, z_lo: 2; z = z_hi * 2 + z_lo), core: 2. Of those that a mesh axis runs over, the one named last changes fastest.
Arguments:
- partials: bfloat16 [32, 8, 256, 4096], P('segment', 'tp'), may hold values from -6 to 6
- residual: bfloat16 [32, 256, 4096], P('segment', 'tp'), may hold values from -80 to 80
- norm_gain: float32 [32, 4096], P('segment'), may hold values from 0.1 to 1.9
- w_query: bfloat16 [32, 4096, 8, 8, 128], P('segment', None, 'tp'), may hold values from -12 to 12
- w_keyval: bfloat16 [32, 4096, 8, 2, 128], P('segment', None, 'tp'), may hold values from -1 to 1
Outputs:
- attended: bfloat16 [32, 256, 8, 8, 128], P('segment', None, 'tp')
The draws below stay inside these ranges and needn't reach their ends.
All inputs are finite; a program needn't handle non-finite values.
Results may differ from the reference program's by a relative error of at most 0.03.
Values may be sent and summed in bfloat16 or wider, within the bound.
No kernel may reach another device: no remote copies, remote signals or barrier semaphores. Data moves between devices by JAX's collectives and lax.ppermute only.
A program may use at most 128 MiB of HBM per device.

```python
import math
import jax
import jax.numpy as jnp
from jax import lax

D = 4096
HEAD_DIM = 128
GROUP = 8
KV_HEADS = 8
TOKENS = 256
SECTIONS = 32
N_TP = 8


def key_weights(key):
    drawn = jax.random.normal(key, (SECTIONS, D, KV_HEADS, HEAD_DIM), jnp.float32)
    return jnp.clip(drawn, -6.0, 6.0) * D ** (-0.5)


def draw_w_keyval(key, part):
    shared = key_weights(key)
    key = jax.random.fold_in(key, 11)
    values = jnp.clip(jax.random.normal(key, (SECTIONS, D, KV_HEADS, HEAD_DIM), jnp.float32), -6.0, 6.0) * D ** (-0.5)
    return jnp.stack([shared, values], axis=3).astype(jnp.bfloat16)


def draw_w_query(key, part):
    key = jax.random.fold_in(key, 12)
    fresh = jnp.clip(jax.random.normal(key, (SECTIONS, D, KV_HEADS, GROUP, HEAD_DIM), jnp.float32), -6.0, 6.0) * D ** (-0.5)
    return fresh.astype(jnp.bfloat16)


def draw_residual(key, part):
    key = jax.random.fold_in(key, 13)
    base_key, scale_key = jax.random.split(key)
    base = jnp.clip(jax.random.normal(base_key, (SECTIONS, TOKENS, D), jnp.float32), -4.0, 4.0)
    scales = jnp.exp(jax.random.uniform(scale_key, (SECTIONS, TOKENS, 1), jnp.float32, 0.0, 2.302585))
    return (base * scales).astype(jnp.bfloat16)


def level_of(stream_key, dims, cuts, smallest, largest):
    gain = 1.0
    for dim, blocks in cuts:
        steps = jax.random.uniform(jax.random.fold_in(jax.random.fold_in(stream_key, 6), dim), (blocks,), jnp.float32, smallest / len(cuts), largest / len(cuts))
        gain = gain * jnp.repeat(jnp.exp(steps), dims[dim] // blocks).reshape((-1,) + (1,) * (len(dims) - 1 - dim))
    return gain


def noise(own_key, extent, deviation, most, pieces=(), kind=jnp.bfloat16):
    entries = deviation * jax.random.normal(own_key, extent, jnp.float32)
    if pieces:
        entries = entries * level_of(own_key, extent, pieces, -0.22, 0.18)
    return jnp.clip(entries, -most, most).astype(kind)


def setup_inputs(seed: int = 0) -> dict:
    key_of = jax.random.split(jax.random.key(seed), 6)
    return {
        "partials": noise(key_of[0], (SECTIONS, N_TP, TOKENS, D), 1.0, 6.0, ((0, 32), (1, 8))),
        "residual": draw_residual(jax.random.fold_in(key_of[5], 71), 0),
        "norm_gain": jnp.clip(1.0 + 0.18 * jax.random.normal(key_of[2], (SECTIONS, D), jnp.float32), 0.1, 1.9),
        "w_query": draw_w_query(jax.random.fold_in(key_of[5], 71), 0),
        "w_keyval": draw_w_keyval(jax.random.fold_in(key_of[5], 71), 0),
    }


ROPE_BASE = 500000.0
NORM_EPS = 1e-05

def rotate(stacked, positions):
    half_dim = stacked.shape[-1] // 2
    frequency = ROPE_BASE ** (-jnp.arange(half_dim, dtype=jnp.float32) * 2.0 / stacked.shape[-1])
    angles = positions[:, None] * frequency[None, :]
    angles = angles.reshape((stacked.shape[0],) + (1,) * (stacked.ndim - 2) + (half_dim,))
    cosine = jnp.cos(angles)
    sine_part = jnp.sin(angles)
    first_half = stacked[..., :half_dim]
    second_half = stacked[..., half_dim:]
    return jnp.concatenate([first_half * cosine - second_half * sine_part, second_half * cosine + first_half * sine_part], axis=-1)

def normalize(stream_rows, gain_row):
    values_f = stream_rows.astype(jnp.float32)
    mean_sq = lax.optimization_barrier(jnp.mean(values_f * values_f, axis=-1, keepdims=True))
    return (values_f * lax.rsqrt(mean_sq + NORM_EPS) * gain_row[None, :]).astype(jnp.bfloat16)

def attend(normed, query_matrix, keyval_matrix):
    model_width, kv_count, group_size, head_dim = query_matrix.shape
    token_count = normed.shape[0]
    queries = jnp.dot(normed, query_matrix.reshape(model_width, -1), preferred_element_type=jnp.float32)
    queries = queries.reshape(token_count, kv_count, group_size, head_dim)
    key_value = jnp.dot(normed, keyval_matrix.reshape(model_width, -1), preferred_element_type=jnp.float32)
    key_value = key_value.reshape(token_count, kv_count, 2, head_dim)
    positions = jnp.arange(token_count).astype(jnp.float32)
    queries = rotate(queries, positions).astype(jnp.bfloat16)
    keys_rot = rotate(key_value[:, :, 0], positions).astype(jnp.bfloat16)
    values = key_value[:, :, 1].astype(jnp.bfloat16)
    scores = jnp.einsum('tkgd,skd->kgts', queries.astype(jnp.float32), keys_rot.astype(jnp.float32)) / math.sqrt(head_dim)
    index_row = jnp.arange(token_count)
    causal = index_row[:, None] >= index_row[None, :]
    scores = jnp.where(causal[None, None], scores, -jnp.inf)
    attn_weights = jax.nn.softmax(scores, axis=-1).astype(jnp.bfloat16)
    attended = jnp.einsum('kgts,skd->tkgd', attn_weights.astype(jnp.float32), values.astype(jnp.float32))
    return attended.astype(jnp.bfloat16)

def reference(partials, residual, norm_gain, w_query, w_keyval):

    def combine(section_pair):
        partial_rows, residual_rows = section_pair
        total = residual_rows.astype(jnp.float32) + lax.optimization_barrier(jnp.sum(partial_rows.astype(jnp.float32), axis=0))
        return total.astype(jnp.bfloat16)
    made = lax.map(combine, (partials, residual))
    stream = jnp.roll(made, 1, axis=0)

    def section(section_items):
        stream_rows, gain_row, query_matrix, keyval_matrix = section_items
        return attend(normalize(stream_rows, gain_row), query_matrix, keyval_matrix)
    return lax.map(section, (stream, norm_gain, w_query, w_keyval))
```

```python
import functools
import math

import jax
import jax.numpy as jnp
from jax import lax
from jax.experimental import pallas as pl
from jax.experimental.pallas import tpu as pltpu
from jax.sharding import PartitionSpec as P

ROPE_BASE = 500000.0
NORM_EPS = 1e-05
CHIPS = 4
CORES = 2


def hop(value, chips, flip):
    pairs = []
    for rank in range(CHIPS * CORES):
        chip, core = divmod(rank, CORES)
        pairs.append((rank, (chip + chips) % CHIPS * CORES + (core ^ flip)))
    return lax.ppermute(value, "tp", pairs)


def next_section(value):
    count = lax.axis_size("segment")
    return lax.ppermute(value, "segment", [(s, (s + 1) % count) for s in range(count)])


def add(*terms):
    return sum(term.astype(jnp.float32) for term in terms).astype(jnp.bfloat16)


def rope(x, cosine, sine):
    half = x.shape[-1] // 2
    return x * cosine + pltpu.roll(x, half, 1) * sine


def attend_kernel(place_ref, own0, own1, own3, own2a, own2b, oth0, oth1, oth3, oth2a, oth2b,
                  cos_ref, sin_ref, wkv_ref, wq_ref, out_ref, rows, keys, values, heads):
    step = pl.program_id(0)
    head_dim = keys.shape[1]

    @pl.when(step == 0)
    def _():
        chip, core = place_ref[0], place_ref[1]
        for mine, (p0, p1, p3, p2a, p2b) in (
            (core, (own0, own1, own3, own2a, own2b)),
            (1 - core, (oth0, oth1, oth3, oth2a, oth2b)),
        ):
            for ahead, low, piece in ((0, 0, p0), (1, 0, p1), (3, 0, p3), (2, 0, p2a), (2, 16, p2b)):
                start = lax.rem(chip + ahead, CHIPS) * 64 + mine * 32 + low
                rows[pl.ds(pl.multiple_of(start, 16), piece.shape[0]), :] = piece[...]
        kv = jnp.dot(rows[...], wkv_ref[...], preferred_element_type=jnp.float32)
        keys[...] = rope(kv[:, :head_dim], cos_ref[...], sin_ref[...]).astype(jnp.bfloat16)
        values[...] = kv[:, head_dim:].astype(jnp.bfloat16)

    q = jnp.dot(rows[...], wq_ref[...], preferred_element_type=jnp.float32)
    tokens = q.shape[0]
    causal = lax.broadcasted_iota(jnp.int32, (tokens, tokens), 0) >= lax.broadcasted_iota(
        jnp.int32, (tokens, tokens), 1
    )
    per_step = q.shape[1] // head_dim
    for h in range(per_step):
        qh = rope(q[:, h * head_dim:(h + 1) * head_dim], cos_ref[...], sin_ref[...]).astype(jnp.bfloat16)
        scores = lax.dot_general(
            qh, keys[...], (((1,), (1,)), ((), ())), preferred_element_type=jnp.float32
        ) * (1.0 / math.sqrt(head_dim))
        scores = jnp.where(causal, scores, -jnp.inf)
        weights = jnp.exp(scores - jnp.max(scores, axis=-1, keepdims=True))
        probs = (weights / jnp.sum(weights, axis=-1, keepdims=True)).astype(jnp.bfloat16)
        heads[step * per_step + h] = jnp.dot(probs, values[...], preferred_element_type=jnp.float32)

    @pl.when(step == pl.num_programs(0) - 1)
    def _():
        for h in range(heads.shape[0]):
            out_ref[:, h, :] = heads[h].astype(jnp.bfloat16)


def per_device(partials, residual, norm_gain, w_query, w_keyval):
    tokens, width = partials.shape[2:]
    group, head_dim = w_query.shape[3:]
    rank = lax.axis_index("tp")
    chip, core = rank // CORES, rank % CORES
    blocks = partials[0, 0].reshape(CHIPS, CORES, tokens // (CHIPS * CORES), width)

    def block(ahead, which):
        return lax.dynamic_slice(
            blocks, (lax.rem(chip + ahead, CHIPS), which, 0, 0), (1, 1) + blocks.shape[2:]
        )[0, 0]

    far = add(block(2, core), hop(block(2, 1 - core), 0, 1))
    rest = hop(jnp.stack([block(d, 1 - core) for d in (1, 3, 0)]), 0, 1)
    up, down, here = (add(block(d, core), rest[i]) for i, d in enumerate((1, 3, 0)))
    low, high = hop(far[:16], 1, 0), hop(far[16:], -1, 0)
    from_below = hop(jnp.concatenate([add(up[:16], low), up[16:]]), 1, 0)
    from_above = hop(jnp.concatenate([down[:16], add(down[16:], high)]), -1, 0)
    made = add(here, from_below, from_above, residual[0])
    stream = next_section(made).astype(jnp.float32)
    mean_sq = jnp.mean(stream * stream, axis=-1, keepdims=True)
    own0 = (stream * lax.rsqrt(mean_sq + NORM_EPS) * norm_gain).astype(jnp.bfloat16)
    oth0 = hop(own0, 0, 1)
    own3, own1 = hop(own0, 1, 0), hop(own0, -1, 0)
    oth3, oth1 = hop(own3, 0, 1), hop(own1, 0, 1)
    own2a, own2b = hop(own3[:16], 1, 0), hop(own1[16:], -1, 0)
    oth2a, oth2b = hop(own2a, 0, 1), hop(own2b, 0, 1)

    half = head_dim // 2
    frequency = ROPE_BASE ** (-jnp.arange(half, dtype=jnp.float32) * 2.0 / head_dim)
    angles = jnp.arange(tokens).astype(jnp.float32)[:, None] * frequency[None, :]
    cosine = jnp.concatenate([jnp.cos(angles)] * 2, axis=1)
    sine = jnp.concatenate([-jnp.sin(angles), jnp.sin(angles)], axis=1)
    wq = w_query.reshape(width, group * head_dim)
    wkv = w_keyval.reshape(width, 2 * head_dim)
    place = jnp.stack([chip, core]).astype(jnp.int32)

    steps = group // 2
    whole = lambda shape: pl.BlockSpec(shape, lambda j, *_: (0,) * len(shape))
    pieces = (own0, own1, own3, own2a, own2b, oth0, oth1, oth3, oth2a, oth2b)
    attended = pl.pallas_call(
        attend_kernel,
        grid_spec=pltpu.PrefetchScalarGridSpec(
            num_scalar_prefetch=1,
            grid=(steps,),
            in_specs=[whole(p.shape) for p in pieces]
            + [whole(cosine.shape), whole(sine.shape), whole(wkv.shape),
               pl.BlockSpec((width, 2 * head_dim), lambda j, *_: (0, j))],
            out_specs=whole((tokens, group, head_dim)),
            scratch_shapes=[
                pltpu.VMEM((tokens, width), jnp.bfloat16),
                pltpu.VMEM((tokens, head_dim), jnp.bfloat16),
                pltpu.VMEM((tokens, head_dim), jnp.bfloat16),
                pltpu.VMEM((group, tokens, head_dim), jnp.float32),
            ],
        ),
        out_shape=jax.ShapeDtypeStruct((tokens, group, head_dim), jnp.bfloat16),
        compiler_params=pltpu.CompilerParams(vmem_limit_bytes=32 * 2**20),
        cost_estimate=pl.CostEstimate(
            flops=2 * tokens * width * (group + 2) * head_dim, bytes_accessed=14 * 2**20, transcendentals=0
        ),
    )(place, *pieces, cosine, sine, wkv, wq)
    return attended.reshape(1, tokens, 1, group, head_dim)


def solution(mesh):
    placed = (
        P("segment", "tp", None, None),
        P("segment", "tp", None),
        P("segment", None),
        P("segment", None, "tp", None, None),
        P("segment", None, "tp", None, None),
    )
    return jax.shard_map(
        per_device,
        mesh=mesh,
        in_specs=placed,
        out_specs=P("segment", None, "tp", None, None),
        check_vma=False,
    )
```

```python
import functools
import math

import jax
import jax.numpy as jnp
from jax import lax
from jax.experimental import pallas as pl
from jax.experimental.pallas import tpu as pltpu
from jax.sharding import PartitionSpec as P

ROPE_BASE = 500000.0
NORM_EPS = 1e-05
CHIPS = 4
CORES = 2
FOLD = 16


def partner(step, chip, core):
    return chip ^ 1 if core == step else CHIPS - 1 - chip


def send(value, step=None, flip=0, sections=(0, 0), cores=(0, 1)):
    ranks = CHIPS * CORES
    count = lax.axis_size("segment")
    pairs = []
    for rank in range(ranks):
        chip, core = divmod(rank, CORES)
        chip = chip if step is None else partner(step, chip, core)
        if core in cores:
            pairs.append((rank, chip * CORES + (core ^ flip), sections[core]))
    if not any(sections):
        return lax.ppermute(value, "tp", [pair[:2] for pair in pairs])
    both = [(s * ranks + a, (s + ahead) % count * ranks + b) for s in range(count) for a, b, ahead in pairs]
    return lax.ppermute(value, ("segment", "tp"), both)


IN_VMEM = pl.BlockSpec(memory_space=pltpu.VMEM)
IN_SMEM = pl.BlockSpec(memory_space=pltpu.SMEM)
IN_HBM = pl.BlockSpec(memory_space=pltpu.HBM)
ANYWHERE = pl.BlockSpec(memory_space=pl.ANY)


def total(*terms):
    return sum(term.astype(jnp.float32) for term in terms)


def sum_kernel(count, *refs):
    refs[-1][...] = total(*(ref[...] for ref in refs[:count])).astype(refs[-1].dtype)


def sum_after(terms, *earlier):
    return pl.pallas_call(
        functools.partial(sum_kernel, len(terms)),
        in_specs=[IN_VMEM] * len(terms) + [ANYWHERE] * len(earlier),
        out_specs=IN_VMEM,
        out_shape=jax.ShapeDtypeStruct(terms[0].shape, jnp.bfloat16),
        compiler_params=pltpu.CompilerParams(vmem_limit_bytes=4 * 2**20),
    )(*terms, *earlier)


def rope(x, cosine, sine):
    return x * cosine + pltpu.roll(x, x.shape[-1] // 2, 1) * sine


def weights_kernel(wq_in, wkv_in, gain_ref, *refs):
    wq_out, wkv_out = refs[-2:]
    gain = gain_ref[...]
    for source, target in ((wq_in, wq_out), (wkv_in, wkv_out)):
        target[...] = (source[...].reshape(target.shape).astype(jnp.float32) * gain).astype(jnp.bfloat16)


def fold_weights(w_query, w_keyval, gain, *earlier):
    width, group, head_dim = w_query.shape
    depth = 512
    return pl.pallas_call(
        weights_kernel,
        grid=(width // depth,),
        in_specs=[
            pl.BlockSpec((depth, group, head_dim), lambda i: (i, 0, 0)),
            pl.BlockSpec((depth, 2, head_dim), lambda i: (i, 0, 0)),
            pl.BlockSpec((depth, 1), lambda i: (i, 0)),
        ]
        + [ANYWHERE] * len(earlier),
        out_specs=[
            pl.BlockSpec((depth, group * head_dim), lambda i: (i, 0)),
            pl.BlockSpec((depth, 2 * head_dim), lambda i: (i, 0)),
        ],
        out_shape=[
            pltpu.VMEM((width, group * head_dim), jnp.bfloat16),
            pltpu.VMEM((width, 2 * head_dim), jnp.bfloat16),
        ],
        compiler_params=pltpu.CompilerParams(vmem_limit_bytes=FOLD * 2**20),
        cost_estimate=pl.CostEstimate(flops=0, bytes_accessed=20 * 2**20, transcendentals=0),
    )(w_query, w_keyval, gain, *earlier)


def attend_kernel(place_ref, *refs):
    pieces, rest = refs[:8], refs[8:]
    cosq, sinq, cosk, sink, wkv_ref, wq_ref, out_ref, rows, queries, heads = rest
    tokens, width = rows.shape
    group, head_dim = out_ref.shape[1:]
    chip, core, one, two = place_ref[0], place_ref[1], place_ref[2], place_ref[3]
    per = pieces[0].shape[0]
    chips = (chip, chip, two, one, one, two, chip ^ 2, chip ^ 2)
    for index, (at, piece) in enumerate(zip(chips, pieces)):
        start = (at * CORES + (core ^ (index % CORES))) * per
        rows[pl.ds(pl.multiple_of(start, per), per), :] = piece[...]
    x = rows[...]
    squares = jnp.sum(jnp.square(x.astype(jnp.float32)), axis=-1, keepdims=True)
    scale = lax.rsqrt(squares * (1.0 / width) + NORM_EPS)
    kv = jnp.dot(x, wkv_ref[...], preferred_element_type=jnp.float32) * scale
    keys = rope(kv[:, :head_dim], cosk[...], sink[...]).astype(jnp.bfloat16)
    ones = jnp.ones((tokens, head_dim), jnp.bfloat16)
    values = jnp.concatenate([kv[:, head_dim:].astype(jnp.bfloat16), ones], axis=1)
    for pair in range(group // 2):
        cols = slice(pair * 2 * head_dim, (pair + 1) * 2 * head_dim)
        q = jnp.dot(x, wq_ref[:, cols], preferred_element_type=jnp.float32) * scale
        for h in range(2):
            turned = rope(q[:, h * head_dim:(h + 1) * head_dim], cosq[...], sinq[...])
            queries[pl.ds((2 * pair + h) * tokens, tokens), :] = turned.astype(jnp.bfloat16)
    causal = lax.broadcasted_iota(jnp.int32, (tokens, tokens), 0) >= lax.broadcasted_iota(
        jnp.int32, (tokens, tokens), 1
    )
    batch = 4
    causal = jnp.concatenate([causal] * batch, axis=0)
    for first in range(0, group, batch):
        scores = lax.dot_general(
            queries[pl.ds(first * tokens, batch * tokens), :], keys, (((1,), (1,)), ((), ())),
            preferred_element_type=jnp.float32,
        )
        scores = jnp.where(causal, scores, -jnp.inf)
        weights = jnp.exp2(scores - jnp.max(scores, axis=-1, keepdims=True)).astype(jnp.bfloat16)
        summed = jnp.dot(weights, values, preferred_element_type=jnp.float32)
        result = summed[:, :head_dim] / summed[:, head_dim:]
        for h in range(batch):
            heads[:, first + h, :] = result[h * tokens:(h + 1) * tokens]
    out_ref[...] = heads[...].astype(jnp.bfloat16)


def per_device(partials, residual, norm_gain, w_query, w_keyval):
    tokens, width = partials.shape[2:]
    group, head_dim = w_query.shape[3:]
    rank = lax.axis_index("tp")
    chip, core = rank >> 1, rank & 1
    blocks = partials[0, 0].reshape(CHIPS, CORES, tokens // (CHIPS * CORES), width)

    one = jnp.where(core == 0, chip ^ 1, CHIPS - 1 - chip)
    two = jnp.where(core == 0, CHIPS - 1 - chip, chip ^ 1)

    def block(at_chip, at_core):
        return lax.dynamic_slice(blocks, (at_chip, at_core, 0, 0), (1, 1) + blocks.shape[2:])[0, 0]

    place = jnp.stack([chip, core, one, two]).astype(jnp.int32)
    far_in = send(block(chip ^ 2, 1 - core), flip=1)
    one_in, two_in, here_in = (send(block(at, 1 - core), flip=1) for at in (two, one, chip))
    far_mine, one_mine, two_mine, here_mine = (block(at, core) for at in (chip ^ 2, one, two, chip))
    far_out = sum_after((far_mine, far_in))
    far = send(far_out, step=0)
    here = send(sum_after((here_mine, here_in, residual[0])), sections=(1, 1))
    near = send(sum_after((one_mine, one_in)), step=0, sections=(1, 1))
    last = send(sum_after((two_mine, two_in, far)), step=1, sections=(1, 1))
    made = sum_after((here, near, last))

    half = head_dim // 2
    frequency = ROPE_BASE ** (-jnp.arange(half, dtype=jnp.float32) * 2.0 / head_dim)
    angles = jnp.arange(tokens).astype(jnp.float32)[:, None] * frequency[None, :]
    cosine = jnp.concatenate([jnp.cos(angles)] * 2, axis=1)
    sine = jnp.concatenate([-jnp.sin(angles), jnp.sin(angles)], axis=1)
    fold = math.log2(math.e) / math.sqrt(head_dim)
    tables = (cosine * fold, sine * fold, cosine, sine)

    own2 = send(made, step=1)
    wq, wkv = fold_weights(w_query[0, :, 0], w_keyval[0, :, 0], norm_gain.reshape(width, 1), made)
    own1 = send(sum_after((made,), wq, wkv, *tables), step=0)
    own0 = made
    own3 = send(own2, step=0)
    pieces = []
    for piece in (own0, own2, own1, own3):
        pieces += [piece, send(piece, flip=1)]

    operands = (*pieces, *tables, wkv, wq)
    attended = pl.pallas_call(
        attend_kernel,
        in_specs=[IN_SMEM] + [IN_VMEM] * len(operands),
        out_specs=IN_VMEM,
        scratch_shapes=[
            pltpu.VMEM((tokens, width), jnp.bfloat16),
            pltpu.VMEM((group * tokens, head_dim), jnp.bfloat16),
            pltpu.VMEM((tokens, group, head_dim), jnp.float32),
        ],
        out_shape=jax.ShapeDtypeStruct((tokens, group, head_dim), jnp.bfloat16),
        compiler_params=pltpu.CompilerParams(vmem_limit_bytes=24 * 2**20),
        cost_estimate=pl.CostEstimate(
            flops=2 * tokens * width * (group + 2) * head_dim, bytes_accessed=14 * 2**20, transcendentals=0
        ),
    )(place, *operands)
    return attended.reshape(1, tokens, 1, group, head_dim)


def solution(mesh):
    placed = (
        P("segment", "tp", None, None),
        P("segment", "tp", None),
        P("segment", None),
        P("segment", None, "tp", None, None),
        P("segment", None, "tp", None, None),
    )
    return jax.shard_map(
        per_device,
        mesh=mesh,
        in_specs=placed,
        out_specs=P("segment", None, "tp", None, None),
        check_vma=False,
    )
```

```python
import functools
import math

import jax
import jax.numpy as jnp
from jax import lax
from jax.experimental import pallas as pl
from jax.experimental.pallas import tpu as pltpu
from jax.sharding import PartitionSpec as P

ROPE_BASE = 500000.0
NORM_EPS = 1e-05
CHIPS = 4
CORES = 2
FOLD = 16


def partner(step, chip, core):
    return chip ^ 1 if core == step else CHIPS - 1 - chip


def send(value, step=None, flip=0, sections=(0, 0), cores=(0, 1)):
    ranks = CHIPS * CORES
    count = lax.axis_size("segment")
    pairs = []
    for rank in range(ranks):
        chip, core = divmod(rank, CORES)
        chip = chip if step is None else partner(step, chip, core)
        if core in cores:
            pairs.append((rank, chip * CORES + (core ^ flip), sections[core]))
    if not any(sections):
        return lax.ppermute(value, "tp", [pair[:2] for pair in pairs])
    both = [(s * ranks + a, (s + ahead) % count * ranks + b) for s in range(count) for a, b, ahead in pairs]
    return lax.ppermute(value, ("segment", "tp"), both)


IN_VMEM = pl.BlockSpec(memory_space=pltpu.VMEM)
IN_SMEM = pl.BlockSpec(memory_space=pltpu.SMEM)
IN_HBM = pl.BlockSpec(memory_space=pltpu.HBM)
ANYWHERE = pl.BlockSpec(memory_space=pl.ANY)


def total(*terms):
    return sum(term.astype(jnp.float32) for term in terms)


def sum_kernel(count, *refs):
    refs[-1][...] = total(*(ref[...] for ref in refs[:count])).astype(refs[-1].dtype)


def sum_after(terms, *earlier):
    return pl.pallas_call(
        functools.partial(sum_kernel, len(terms)),
        in_specs=[IN_VMEM] * len(terms) + [ANYWHERE] * len(earlier),
        out_specs=IN_VMEM,
        out_shape=jax.ShapeDtypeStruct(terms[0].shape, jnp.bfloat16),
        compiler_params=pltpu.CompilerParams(vmem_limit_bytes=4 * 2**20),
    )(*terms, *earlier)


def rope(x, cosine, sine):
    return x * cosine + pltpu.roll(x, x.shape[-1] // 2, 1) * sine


def weights_kernel(wq_in, wkv_in, gain_ref, *refs):
    wq_out, wkv_out = refs[-2:]
    gain = gain_ref[...]
    for source, target in ((wq_in, wq_out), (wkv_in, wkv_out)):
        target[...] = (source[...].reshape(target.shape).astype(jnp.float32) * gain).astype(jnp.bfloat16)


def fold_weights(w_query, w_keyval, gain, *earlier):
    width, group, head_dim = w_query.shape
    depth = 512
    return pl.pallas_call(
        weights_kernel,
        grid=(width // depth,),
        in_specs=[
            pl.BlockSpec((depth, group, head_dim), lambda i: (i, 0, 0)),
            pl.BlockSpec((depth, 2, head_dim), lambda i: (i, 0, 0)),
            pl.BlockSpec((depth, 1), lambda i: (i, 0)),
        ]
        + [ANYWHERE] * len(earlier),
        out_specs=[
            pl.BlockSpec((depth, group * head_dim), lambda i: (i, 0)),
            pl.BlockSpec((depth, 2 * head_dim), lambda i: (i, 0)),
        ],
        out_shape=[
            pltpu.VMEM((width, group * head_dim), jnp.bfloat16),
            pltpu.VMEM((width, 2 * head_dim), jnp.bfloat16),
        ],
        compiler_params=pltpu.CompilerParams(vmem_limit_bytes=FOLD * 2**20),
        cost_estimate=pl.CostEstimate(flops=0, bytes_accessed=20 * 2**20, transcendentals=0),
    )(w_query, w_keyval, gain, *earlier)


def attend_kernel(place_ref, *refs):
    pieces, rest = refs[:8], refs[8:]
    cosq, sinq, cosk, sink, wkv_ref, wq_ref, out_ref, rows, queries, heads = rest
    tokens, width = rows.shape
    group, head_dim = out_ref.shape[1:]
    chip, core, one, two = place_ref[0], place_ref[1], place_ref[2], place_ref[3]
    per = pieces[0].shape[0]
    chips = (chip, chip, two, one, one, two, chip ^ 2, chip ^ 2)
    for index, (at, piece) in enumerate(zip(chips, pieces)):
        start = (at * CORES + (core ^ (index % CORES))) * per
        rows[pl.ds(pl.multiple_of(start, per), per), :] = piece[...]
    x = rows[...]
    squares = jnp.sum(jnp.square(x.astype(jnp.float32)), axis=-1, keepdims=True)
    scale = lax.rsqrt(squares * (1.0 / width) + NORM_EPS)
    kv = jnp.dot(x, wkv_ref[...], preferred_element_type=jnp.float32) * scale
    keys = rope(kv[:, :head_dim], cosk[...], sink[...]).astype(jnp.bfloat16)
    ones = jnp.ones((tokens, head_dim), jnp.bfloat16)
    values = jnp.concatenate([kv[:, head_dim:].astype(jnp.bfloat16), ones], axis=1)
    for pair in range(group // 2):
        cols = slice(pair * 2 * head_dim, (pair + 1) * 2 * head_dim)
        q = jnp.dot(x, wq_ref[:, cols], preferred_element_type=jnp.float32) * scale
        for h in range(2):
            turned = rope(q[:, h * head_dim:(h + 1) * head_dim], cosq[...], sinq[...])
            queries[pl.ds((2 * pair + h) * tokens, tokens), :] = turned.astype(jnp.bfloat16)
    causal = lax.broadcasted_iota(jnp.int32, (tokens, tokens), 0) >= lax.broadcasted_iota(
        jnp.int32, (tokens, tokens), 1
    )
    batch = 4
    causal = jnp.concatenate([causal] * batch, axis=0)
    for first in range(0, group, batch):
        scores = lax.dot_general(
            queries[pl.ds(first * tokens, batch * tokens), :], keys, (((1,), (1,)), ((), ())),
            preferred_element_type=jnp.float32,
        )
        scores = jnp.where(causal, scores, -jnp.inf)
        weights = jnp.exp2(scores - jnp.max(scores, axis=-1, keepdims=True)).astype(jnp.bfloat16)
        summed = jnp.dot(weights, values, preferred_element_type=jnp.float32)
        result = summed[:, :head_dim] / summed[:, head_dim:]
        for h in range(batch):
            heads[:, first + h, :] = result[h * tokens:(h + 1) * tokens]
    out_ref[...] = heads[...].astype(jnp.bfloat16)


def per_device(partials, residual, norm_gain, w_query, w_keyval):
    tokens, width = partials.shape[2:]
    group, head_dim = w_query.shape[3:]
    rank = lax.axis_index("tp")
    chip, core = rank >> 1, rank & 1
    blocks = partials[0, 0].reshape(CHIPS, CORES, tokens // (CHIPS * CORES), width)

    one = jnp.where(core == 0, chip ^ 1, CHIPS - 1 - chip)
    two = jnp.where(core == 0, CHIPS - 1 - chip, chip ^ 1)

    def block(at_chip, at_core):
        return lax.dynamic_slice(blocks, (at_chip, at_core, 0, 0), (1, 1) + blocks.shape[2:])[0, 0]

    place = jnp.stack([chip, core, one, two]).astype(jnp.int32)
    far_in = send(block(chip ^ 2, 1 - core), flip=1)
    one_in, two_in, here_in = (send(block(at, 1 - core), flip=1) for at in (two, one, chip))
    far_mine, one_mine, two_mine, here_mine = (block(at, core) for at in (chip ^ 2, one, two, chip))
    far_out = sum_after((far_mine, far_in))
    far = send(far_out, step=0)
    near = send(sum_after((one_mine, one_in)), step=0)
    last = send(sum_after((two_mine, two_in, far)), step=1, sections=(1, 1))
    here = send(sum_after((here_mine, here_in, near, residual[0])), sections=(1, 1))
    made = sum_after((here, last))

    half = head_dim // 2
    frequency = ROPE_BASE ** (-jnp.arange(half, dtype=jnp.float32) * 2.0 / head_dim)
    angles = jnp.arange(tokens).astype(jnp.float32)[:, None] * frequency[None, :]
    cosine = jnp.concatenate([jnp.cos(angles)] * 2, axis=1)
    sine = jnp.concatenate([-jnp.sin(angles), jnp.sin(angles)], axis=1)
    fold = math.log2(math.e) / math.sqrt(head_dim)
    tables = (cosine * fold, sine * fold, cosine, sine)

    own2 = send(made, step=1)
    wq, wkv = fold_weights(w_query[0, :, 0], w_keyval[0, :, 0], norm_gain.reshape(width, 1), made)
    own1 = send(sum_after((made,), wq, wkv, *tables), step=0)
    own0 = made
    own3 = send(own2, step=0)
    pieces = []
    for piece in (own0, own2, own1, own3):
        pieces += [piece, send(piece, flip=1)]

    operands = (*pieces, *tables, wkv, wq)
    attended = pl.pallas_call(
        attend_kernel,
        in_specs=[IN_SMEM] + [IN_VMEM] * len(operands),
        out_specs=IN_VMEM,
        scratch_shapes=[
            pltpu.VMEM((tokens, width), jnp.bfloat16),
            pltpu.VMEM((group * tokens, head_dim), jnp.bfloat16),
            pltpu.VMEM((tokens, group, head_dim), jnp.float32),
        ],
        out_shape=jax.ShapeDtypeStruct((tokens, group, head_dim), jnp.bfloat16),
        compiler_params=pltpu.CompilerParams(vmem_limit_bytes=24 * 2**20),
        cost_estimate=pl.CostEstimate(
            flops=2 * tokens * width * (group + 2) * head_dim, bytes_accessed=14 * 2**20, transcendentals=0
        ),
    )(place, *operands)
    return attended.reshape(1, tokens, 1, group, head_dim)


def solution(mesh):
    placed = (
        P("segment", "tp", None, None),
        P("segment", "tp", None),
        P("segment", None),
        P("segment", None, "tp", None, None),
        P("segment", None, "tp", None, None),
    )
    return jax.shard_map(
        per_device,
        mesh=mesh,
        in_specs=placed,
        out_specs=P("segment", None, "tp", None, None),
        check_vma=False,
    )
```

```python
import functools
import math

import jax
import jax.numpy as jnp
from jax import lax
from jax.experimental import pallas as pl
from jax.experimental.pallas import tpu as pltpu
from jax.sharding import PartitionSpec as P

ROPE_BASE = 500000.0
NORM_EPS = 1e-05
CHIPS = 4
CORES = 2


def partner(step, chip, core):
    return chip ^ 1 if core == step else CHIPS - 1 - chip


def send(value, step=None, flip=0, sections=(0, 0), cores=(0, 1)):
    ranks = CHIPS * CORES
    count = lax.axis_size("segment")
    pairs = []
    for rank in range(ranks):
        chip, core = divmod(rank, CORES)
        chip = chip if step is None else partner(step, chip, core)
        if core in cores:
            pairs.append((rank, chip * CORES + (core ^ flip), sections[core]))
    if not any(sections):
        return lax.ppermute(value, "tp", [pair[:2] for pair in pairs])
    both = [(s * ranks + a, (s + ahead) % count * ranks + b) for s in range(count) for a, b, ahead in pairs]
    return lax.ppermute(value, ("segment", "tp"), both)


IN_VMEM = pl.BlockSpec(memory_space=pltpu.VMEM)
IN_SMEM = pl.BlockSpec(memory_space=pltpu.SMEM)
IN_HBM = pl.BlockSpec(memory_space=pltpu.HBM)
ANYWHERE = pl.BlockSpec(memory_space=pl.ANY)


def total(*terms):
    return sum(term.astype(jnp.float32) for term in terms)


def sum_kernel(count, *refs):
    refs[-1][...] = total(*(ref[...] for ref in refs[:count])).astype(refs[-1].dtype)


def sum_after(terms, *earlier):
    return pl.pallas_call(
        functools.partial(sum_kernel, len(terms)),
        in_specs=[IN_VMEM] * len(terms) + [ANYWHERE] * len(earlier),
        out_specs=IN_VMEM,
        out_shape=jax.ShapeDtypeStruct(terms[0].shape, jnp.bfloat16),
        compiler_params=pltpu.CompilerParams(vmem_limit_bytes=4 * 2**20),
    )(*terms, *earlier)


def normed_kernel(here, last, gain_ref, out_ref):
    stream = total(here[...], last[...]).astype(jnp.bfloat16).astype(jnp.float32)
    mean_sq = jnp.mean(stream * stream, axis=-1, keepdims=True)
    out_ref[...] = (stream * lax.rsqrt(mean_sq + NORM_EPS) * gain_ref[...]).astype(jnp.bfloat16)


def rope(x, cosine, sine):
    return x * cosine + pltpu.roll(x, x.shape[-1] // 2, 1) * sine


def weights_kernel(wq_in, wkv_in, earlier_ref, wq_out, wkv_out):
    wq_out[...] = wq_in[...].reshape(wq_out.shape)
    wkv_out[...] = wkv_in[...].reshape(wkv_out.shape)


def lay_out_weights(w_query, w_keyval, earlier):
    width, group, head_dim = w_query.shape
    depth = 512
    return pl.pallas_call(
        weights_kernel,
        grid=(width // depth,),
        in_specs=[
            pl.BlockSpec((depth, group, head_dim), lambda i: (i, 0, 0)),
            pl.BlockSpec((depth, 2, head_dim), lambda i: (i, 0, 0)),
            ANYWHERE,
        ],
        out_specs=[
            pl.BlockSpec((depth, group * head_dim), lambda i: (i, 0)),
            pl.BlockSpec((depth, 2 * head_dim), lambda i: (i, 0)),
        ],
        out_shape=[
            pltpu.VMEM((width, group * head_dim), jnp.bfloat16),
            pltpu.VMEM((width, 2 * head_dim), jnp.bfloat16),
        ],
        compiler_params=pltpu.CompilerParams(vmem_limit_bytes=16 * 2**20),
        cost_estimate=pl.CostEstimate(flops=0, bytes_accessed=20 * 2**20, transcendentals=0),
    )(w_query, w_keyval, earlier)


def attend_kernel(place_ref, *refs):
    pieces, rest = refs[:8], refs[8:]
    cosq, sinq, cosk, sink, wkv_ref, wq_ref, out_ref, rows, queries, heads = rest
    tokens, width = rows.shape
    group, head_dim = out_ref.shape[1:]
    chip, core, one, two = place_ref[0], place_ref[1], place_ref[2], place_ref[3]
    per = pieces[0].shape[0]
    chips = (chip, chip, two, one, one, two, chip ^ 2, chip ^ 2)
    for index, (at, piece) in enumerate(zip(chips, pieces)):
        start = (at * CORES + (core ^ (index % CORES))) * per
        rows[pl.ds(pl.multiple_of(start, per), per), :] = piece[...]
    x = rows[...]
    kv = jnp.dot(x, wkv_ref[...], preferred_element_type=jnp.float32)
    keys = rope(kv[:, :head_dim], cosk[...], sink[...]).astype(jnp.bfloat16)
    ones = jnp.ones((tokens, head_dim), jnp.bfloat16)
    values = jnp.concatenate([kv[:, head_dim:].astype(jnp.bfloat16), ones], axis=1)
    for pair in range(group // 2):
        cols = slice(pair * 2 * head_dim, (pair + 1) * 2 * head_dim)
        q = jnp.dot(x, wq_ref[:, cols], preferred_element_type=jnp.float32)
        for h in range(2):
            turned = rope(q[:, h * head_dim:(h + 1) * head_dim], cosq[...], sinq[...])
            queries[pl.ds((2 * pair + h) * tokens, tokens), :] = turned.astype(jnp.bfloat16)
    causal = lax.broadcasted_iota(jnp.int32, (tokens, tokens), 0) >= lax.broadcasted_iota(
        jnp.int32, (tokens, tokens), 1
    )
    batch = 4
    causal = jnp.concatenate([causal] * batch, axis=0)
    for first in range(0, group, batch):
        scores = lax.dot_general(
            queries[pl.ds(first * tokens, batch * tokens), :], keys, (((1,), (1,)), ((), ())),
            preferred_element_type=jnp.float32,
        )
        scores = jnp.where(causal, scores, -jnp.inf)
        weights = jnp.exp2(scores - jnp.max(scores, axis=-1, keepdims=True)).astype(jnp.bfloat16)
        summed = jnp.dot(weights, values, preferred_element_type=jnp.float32)
        result = summed[:, :head_dim] / summed[:, head_dim:]
        for h in range(batch):
            heads[:, first + h, :] = result[h * tokens:(h + 1) * tokens]
    out_ref[...] = heads[...].astype(jnp.bfloat16)


def per_device(partials, residual, norm_gain, w_query, w_keyval):
    tokens, width = partials.shape[2:]
    group, head_dim = w_query.shape[3:]
    rank = lax.axis_index("tp")
    chip, core = rank >> 1, rank & 1
    blocks = partials[0, 0].reshape(CHIPS, CORES, tokens // (CHIPS * CORES), width)

    one = jnp.where(core == 0, chip ^ 1, CHIPS - 1 - chip)
    two = jnp.where(core == 0, CHIPS - 1 - chip, chip ^ 1)

    def block(at_chip, at_core):
        return lax.dynamic_slice(blocks, (at_chip, at_core, 0, 0), (1, 1) + blocks.shape[2:])[0, 0]

    place = jnp.stack([chip, core, one, two]).astype(jnp.int32)
    far_in = send(block(chip ^ 2, 1 - core), flip=1)
    one_in, two_in, here_in = (send(block(at, 1 - core), flip=1) for at in (two, one, chip))
    far_mine, one_mine, two_mine, here_mine = (block(at, core) for at in (chip ^ 2, one, two, chip))
    far_out = sum_after((far_mine, far_in))
    far = send(far_out, step=0)
    near = send(sum_after((one_mine, one_in)), step=0)
    last = send(sum_after((two_mine, two_in, far)), step=1, sections=(1, 1))
    here = send(sum_after((here_mine, here_in, near, residual[0])), sections=(1, 1))
    made = pl.pallas_call(
        normed_kernel,
        in_specs=[IN_VMEM] * 3,
        out_specs=IN_VMEM,
        out_shape=jax.ShapeDtypeStruct(here.shape, jnp.bfloat16),
        compiler_params=pltpu.CompilerParams(vmem_limit_bytes=4 * 2**20),
    )(here, last, norm_gain)

    half = head_dim // 2
    frequency = ROPE_BASE ** (-jnp.arange(half, dtype=jnp.float32) * 2.0 / head_dim)
    angles = jnp.arange(tokens).astype(jnp.float32)[:, None] * frequency[None, :]
    cosine = jnp.concatenate([jnp.cos(angles)] * 2, axis=1)
    sine = jnp.concatenate([-jnp.sin(angles), jnp.sin(angles)], axis=1)
    fold = math.log2(math.e) / math.sqrt(head_dim)
    tables = (cosine * fold, sine * fold, cosine, sine)

    own2 = send(made, step=1)
    wq, wkv = lay_out_weights(w_query[0, :, 0], w_keyval[0, :, 0], made)
    own1 = send(sum_after((made,), wq, wkv, *tables), step=0)
    own0 = made
    own3 = send(own2, step=0)
    pieces = []
    for piece in (own0, own2, own1, own3):
        pieces += [piece, send(piece, flip=1)]

    operands = (*pieces, *tables, wkv, wq)
    attended = pl.pallas_call(
        attend_kernel,
        in_specs=[IN_SMEM] + [IN_VMEM] * len(operands),
        out_specs=IN_VMEM,
        scratch_shapes=[
            pltpu.VMEM((tokens, width), jnp.bfloat16),
            pltpu.VMEM((group * tokens, head_dim), jnp.bfloat16),
            pltpu.VMEM((tokens, group, head_dim), jnp.float32),
        ],
        out_shape=jax.ShapeDtypeStruct((tokens, group, head_dim), jnp.bfloat16),
        compiler_params=pltpu.CompilerParams(vmem_limit_bytes=24 * 2**20),
        cost_estimate=pl.CostEstimate(
            flops=2 * tokens * width * (group + 2) * head_dim, bytes_accessed=14 * 2**20, transcendentals=0
        ),
    )(place, *operands)
    return attended.reshape(1, tokens, 1, group, head_dim)


def solution(mesh):
    placed = (
        P("segment", "tp", None, None),
        P("segment", "tp", None),
        P("segment", None),
        P("segment", None, "tp", None, None),
        P("segment", None, "tp", None, None),
    )
    return jax.shard_map(
        per_device,
        mesh=mesh,
        in_specs=placed,
        out_specs=P("segment", None, "tp", None, None),
        check_vma=False,
    )
```

```python
import functools
import math

import jax
import jax.numpy as jnp
from jax import lax
from jax.experimental import pallas as pl
from jax.experimental.pallas import tpu as pltpu
from jax.sharding import PartitionSpec as P

ROPE_BASE = 500000.0
NORM_EPS = 1e-05
CHIPS = 4
CORES = 2


def partner(step, chip, core):
    return chip ^ 1 if core == step else CHIPS - 1 - chip


def send(value, step=None, flip=0, sections=(0, 0), cores=(0, 1)):
    ranks = CHIPS * CORES
    count = lax.axis_size("segment")
    pairs = []
    for rank in range(ranks):
        chip, core = divmod(rank, CORES)
        chip = chip if step is None else partner(step, chip, core)
        if core in cores:
            pairs.append((rank, chip * CORES + (core ^ flip), sections[core]))
    if not any(sections):
        return lax.ppermute(value, "tp", [pair[:2] for pair in pairs])
    both = [(s * ranks + a, (s + ahead) % count * ranks + b) for s in range(count) for a, b, ahead in pairs]
    return lax.ppermute(value, ("segment", "tp"), both)


IN_VMEM = pl.BlockSpec(memory_space=pltpu.VMEM)
IN_SMEM = pl.BlockSpec(memory_space=pltpu.SMEM)
IN_HBM = pl.BlockSpec(memory_space=pltpu.HBM)
ANYWHERE = pl.BlockSpec(memory_space=pl.ANY)


def total(*terms):
    return sum(term.astype(jnp.float32) for term in terms)


def sum_kernel(count, *refs):
    refs[-1][...] = total(*(ref[...] for ref in refs[:count])).astype(refs[-1].dtype)


def sum_after(terms, *earlier):
    return pl.pallas_call(
        functools.partial(sum_kernel, len(terms)),
        in_specs=[IN_VMEM] * len(terms) + [ANYWHERE] * len(earlier),
        out_specs=IN_VMEM,
        out_shape=jax.ShapeDtypeStruct(terms[0].shape, jnp.bfloat16),
        compiler_params=pltpu.CompilerParams(vmem_limit_bytes=4 * 2**20),
    )(*terms, *earlier)


def normed_kernel(here, last, gain_ref, *refs):
    stream = total(here[...], last[...]).astype(jnp.bfloat16).astype(jnp.float32)
    mean_sq = jnp.mean(stream * stream, axis=-1, keepdims=True)
    refs[-1][...] = (stream * lax.rsqrt(mean_sq + NORM_EPS) * gain_ref[...]).astype(jnp.bfloat16)


def rope(x, cosine, sine):
    return x * cosine + pltpu.roll(x, x.shape[-1] // 2, 1) * sine


def weights_kernel(wq_in, wkv_in, earlier_ref, wq_out, wkv_out):
    wq_out[...] = wq_in[...].reshape(wq_out.shape)
    wkv_out[...] = wkv_in[...].reshape(wkv_out.shape)


def lay_out_weights(w_query, w_keyval, earlier):
    width, group, head_dim = w_query.shape
    depth = 512
    return pl.pallas_call(
        weights_kernel,
        grid=(width // depth,),
        in_specs=[
            pl.BlockSpec((depth, group, head_dim), lambda i: (i, 0, 0)),
            pl.BlockSpec((depth, 2, head_dim), lambda i: (i, 0, 0)),
            ANYWHERE,
        ],
        out_specs=[
            pl.BlockSpec((depth, group * head_dim), lambda i: (i, 0)),
            pl.BlockSpec((depth, 2 * head_dim), lambda i: (i, 0)),
        ],
        out_shape=[
            pltpu.VMEM((width, group * head_dim), jnp.bfloat16),
            pltpu.VMEM((width, 2 * head_dim), jnp.bfloat16),
        ],
        compiler_params=pltpu.CompilerParams(vmem_limit_bytes=16 * 2**20),
        cost_estimate=pl.CostEstimate(flops=0, bytes_accessed=20 * 2**20, transcendentals=0),
    )(w_query, w_keyval, earlier)


def attend_kernel(place_ref, *refs):
    pieces, rest = refs[:8], refs[8:]
    cosq, sinq, cosk, sink, wkv_ref, wq_ref, out_ref, rows, queries, heads = rest
    tokens, width = rows.shape
    group, head_dim = out_ref.shape[1:]
    chip, core, one, two = place_ref[0], place_ref[1], place_ref[2], place_ref[3]
    per = pieces[0].shape[0]
    chips = (chip, chip, two, one, one, two, chip ^ 2, chip ^ 2)
    for index, (at, piece) in enumerate(zip(chips, pieces)):
        start = (at * CORES + (core ^ (index % CORES))) * per
        rows[pl.ds(pl.multiple_of(start, per), per), :] = piece[...]
    x = rows[...]
    kv = jnp.dot(x, wkv_ref[...], preferred_element_type=jnp.float32)
    keys = rope(kv[:, :head_dim], cosk[...], sink[...]).astype(jnp.bfloat16)
    ones = jnp.ones((tokens, head_dim), jnp.bfloat16)
    values = jnp.concatenate([kv[:, head_dim:].astype(jnp.bfloat16), ones], axis=1)
    for pair in range(group // 2):
        cols = slice(pair * 2 * head_dim, (pair + 1) * 2 * head_dim)
        q = jnp.dot(x, wq_ref[:, cols], preferred_element_type=jnp.float32)
        for h in range(2):
            turned = rope(q[:, h * head_dim:(h + 1) * head_dim], cosq[...], sinq[...])
            queries[pl.ds((2 * pair + h) * tokens, tokens), :] = turned.astype(jnp.bfloat16)
    causal = lax.broadcasted_iota(jnp.int32, (tokens, tokens), 0) >= lax.broadcasted_iota(
        jnp.int32, (tokens, tokens), 1
    )
    batch = 4
    causal = jnp.concatenate([causal] * batch, axis=0)
    for first in range(0, group, batch):
        scores = lax.dot_general(
            queries[pl.ds(first * tokens, batch * tokens), :], keys, (((1,), (1,)), ((), ())),
            preferred_element_type=jnp.float32,
        )
        scores = jnp.where(causal, scores, -jnp.inf)
        weights = jnp.exp2(scores - jnp.max(scores, axis=-1, keepdims=True)).astype(jnp.bfloat16)
        summed = jnp.dot(weights, values, preferred_element_type=jnp.float32)
        result = summed[:, :head_dim] / summed[:, head_dim:]
        for h in range(batch):
            heads[:, first + h, :] = result[h * tokens:(h + 1) * tokens]
    out_ref[...] = heads[...].astype(jnp.bfloat16)


def per_device(partials, residual, norm_gain, w_query, w_keyval):
    tokens, width = partials.shape[2:]
    group, head_dim = w_query.shape[3:]
    rank = lax.axis_index("tp")
    chip, core = rank >> 1, rank & 1
    blocks = partials[0, 0].reshape(CHIPS, CORES, tokens // (CHIPS * CORES), width)

    one = jnp.where(core == 0, chip ^ 1, CHIPS - 1 - chip)
    two = jnp.where(core == 0, CHIPS - 1 - chip, chip ^ 1)

    def block(at_chip, at_core):
        return lax.dynamic_slice(blocks, (at_chip, at_core, 0, 0), (1, 1) + blocks.shape[2:])[0, 0]

    half = head_dim // 2
    frequency = ROPE_BASE ** (-jnp.arange(half, dtype=jnp.float32) * 2.0 / head_dim)
    angles = jnp.arange(tokens).astype(jnp.float32)[:, None] * frequency[None, :]
    cosine = jnp.concatenate([jnp.cos(angles)] * 2, axis=1)
    sine = jnp.concatenate([-jnp.sin(angles), jnp.sin(angles)], axis=1)
    fold = math.log2(math.e) / math.sqrt(head_dim)
    tables = (cosine * fold, sine * fold, cosine, sine)

    place = jnp.stack([chip, core, one, two]).astype(jnp.int32)
    far_in = send(block(chip ^ 2, 1 - core), flip=1)
    one_in, two_in, here_in = (send(block(at, 1 - core), flip=1) for at in (two, one, chip))
    far_mine, one_mine, two_mine, here_mine = (block(at, core) for at in (chip ^ 2, one, two, chip))
    far_out = sum_after((far_mine, far_in))
    far = send(far_out, step=0)
    near = send(sum_after((one_mine, one_in)), step=0)
    last = send(sum_after((two_mine, two_in, far)), step=1, sections=(1, 1))
    here = send(sum_after((here_mine, here_in, near, residual[0])), sections=(1, 1))
    made = pl.pallas_call(
        normed_kernel,
        in_specs=[IN_VMEM] * 3 + [ANYWHERE] * len(tables),
        out_specs=IN_VMEM,
        out_shape=jax.ShapeDtypeStruct(here.shape, jnp.bfloat16),
        compiler_params=pltpu.CompilerParams(vmem_limit_bytes=4 * 2**20),
    )(here, last, norm_gain, *tables)

    own2 = send(made, step=1)
    wq, wkv = lay_out_weights(w_query[0, :, 0], w_keyval[0, :, 0], made)
    own1 = send(sum_after((made,), wq, wkv), step=0)
    own0 = made
    own3 = send(own2, step=0)
    pieces = []
    for piece in (own0, own2, own1, own3):
        pieces += [piece, send(piece, flip=1)]

    operands = (*pieces, *tables, wkv, wq)
    attended = pl.pallas_call(
        attend_kernel,
        in_specs=[IN_SMEM] + [IN_VMEM] * len(operands),
        out_specs=IN_VMEM,
        scratch_shapes=[
            pltpu.VMEM((tokens, width), jnp.bfloat16),
            pltpu.VMEM((group * tokens, head_dim), jnp.bfloat16),
            pltpu.VMEM((tokens, group, head_dim), jnp.float32),
        ],
        out_shape=jax.ShapeDtypeStruct((tokens, group, head_dim), jnp.bfloat16),
        compiler_params=pltpu.CompilerParams(vmem_limit_bytes=24 * 2**20),
        cost_estimate=pl.CostEstimate(
            flops=2 * tokens * width * (group + 2) * head_dim, bytes_accessed=14 * 2**20, transcendentals=0
        ),
    )(place, *operands)
    return attended.reshape(1, tokens, 1, group, head_dim)


def solution(mesh):
    placed = (
        P("segment", "tp", None, None),
        P("segment", "tp", None),
        P("segment", None),
        P("segment", None, "tp", None, None),
        P("segment", None, "tp", None, None),
    )
    return jax.shard_map(
        per_device,
        mesh=mesh,
        in_specs=placed,
        out_specs=P("segment", None, "tp", None, None),
        check_vma=False,
    )
```
